32 devices in a mesh: dp: 2 (over x), expert: 16 (over z, y, core).
Axes of the slice: x: 2, y: 2, z: 4, core: 2. Of those that a mesh axis runs over, the one named last changes fastest.
Arguments:
- tokens: bfloat16 [5120, 2048], P(('dp', 'expert')), may hold values from -6 to 6
- out_grad: bfloat16 [5120, 2048], P(('dp', 'expert')), may hold values from -6 to 6
- expert_ids: int32 [5120, 8], P(('dp', 'expert')), may hold values from 0 to 127, all different within a row; in each aligned block of 160 rows (0 to 159, 160 to 319, ...) at most 15 rows name the same one
- gate_vals: bfloat16 [5120, 8], P(('dp', 'expert')), may hold values from 0.049804688 to 0.59765625
- w_gate: bfloat16 [16, 2048, 768], P('expert'), may hold values from -0.125 to 0.125
- w_up: bfloat16 [16, 2048, 768], P('expert'), may hold values from -0.125 to 0.125
- w_down: bfloat16 [16, 768, 2048], P('expert'), may hold values from -0.21875 to 0.21875
Outputs:
- d_tokens: bfloat16 [5120, 2048], P(('dp', 'expert'))
- d_gates: bfloat16 [5120, 8], P(('dp', 'expert'))
- d_w_gate: bfloat16 [16, 2048, 768], P('expert', 'dp')
- d_w_up: bfloat16 [16, 2048, 768], P('expert', 'dp')
- d_w_down: bfloat16 [16, 768, 2048], P('expert', None, 'dp')
The draws below stay inside these ranges and needn't reach their ends.
Inputs may be any that keep to these rules, and one draw needn't show every extreme that they name: `expert_ids`: each row names 8 different experts and every expert is named somewhere. Among the 160 rows of one device no expert is named more than 15 times, a bound that some block reaches. Experts 16 and above lie outside this window.
All inputs are finite; a program needn't handle non-finite values.
Results may differ from the reference program's by a relative error of at most 0.012.
Values may be sent and summed in bfloat16 or wider, within the bound.
No kernel may reach another device: no remote copies, remote signals or barrier semaphores. Data moves between devices by JAX's collectives and lax.ppermute only.
A program may use at most 128 MiB of HBM per device.

```python
import math
import jax
import jax.numpy as jnp
import numpy as np
from jax import lax

D = 2048
FF = 768
EXPERTS_ALL = 128
TOPK = 8
EXP_DEV = 1
TOK_DEV = 160
CAP = 15
EXPERTS = 16
TOKENS = 5120
N_DP = 2
N_EXPERT = 16


def levels(rng, dims, shards, smallest, high):
    def one(dim, shards_of):
        heights = jax.random.uniform(jax.random.fold_in(jax.random.fold_in(rng, 6), dim), (shards_of,), jnp.float32, smallest / len(shards), high / len(shards))
        return jnp.repeat(jnp.exp(heights), dims[dim] // shards_of).reshape((-1,) + (1,) * (len(dims) - dim - 1))

    gain = one(*shards[0])
    for cut in shards[1:]:
        gain = gain * one(*cut)
    return gain


def routed_block(stream_key, own, number, rows, number_of, top, limit, lean):
    ranking = jax.random.permutation(stream_key, number_of)
    packed, usual = portions_of(number_of, rows * top, limit, lean, True), portions_of(number_of, rows * top, limit, lean, False)
    places = jnp.arange(number_of)

    def named(sizes, turn):
        used = int((sizes > 0).sum())
        fixed = max(1, used // 4)
        passed = fixed + (places - fixed + turn * (used - fixed)) % max(1, number_of - fixed)
        return jnp.zeros((number_of,), jnp.int32).at[ranking[jnp.where(places < fixed, places, passed)]].set(jnp.asarray(sizes, jnp.int32))

    sizes = jnp.where(number % 4 == 0, named(packed, number // 4), named(usual, number - number // 4 - 1))
    mixed = jax.random.permutation(jax.random.fold_in(own, 3), number_of)
    donor, sink = mixed[0:number_of // 2 * 2:2], mixed[1:number_of // 2 * 2:2]
    room = jnp.minimum(sizes[donor] - 1, limit - sizes[sink]) // 2
    room = jnp.where((donor == ranking[0]) | (sink == ranking[0]) | (sizes[sink] == 0), 0, jnp.maximum(room, 0))
    passed = jax.random.randint(jax.random.fold_in(own, 4), (number_of // 2,), 0, 1 << 20) % (room + 1)
    sizes = sizes.at[donor].add(-passed).at[sink].add(passed)
    members = jnp.searchsorted(jnp.cumsum(sizes), jnp.arange(rows * top), side="right").astype(jnp.int32)
    grid = members.reshape(top, rows).T
    grid = grid[jax.random.permutation(jax.random.fold_in(own, 1), rows)]
    turn = jax.random.randint(jax.random.fold_in(own, 2), (rows, 1), 0, top)
    return jnp.take_along_axis(grid, (jnp.arange(top)[None, :] + turn) % top, axis=1)


def portions_of(count, total, bound, lean, full):
    loads = [(1 << 20) // math.isqrt(rank ** lean) + 1 for rank in range(1, count + 1)]
    largest = bound if full else min(bound, max(-(-total // count), total * loads[0] // sum(loads)))
    least = 1 if total - largest >= count - 1 else 0
    holding, rest = [largest] + [least] * (count - 1), total - largest - least * (count - 1)
    while rest > 0:
        candidates = [i for i in range(1, count) if holding[i] < largest] or [i for i in range(1, count) if holding[i] < bound]
        pool, remaining = sum([loads[i] for i in candidates]), rest
        for i in candidates:
            addition = min(bound - holding[i], max(1, remaining * loads[i] // pool), rest)
            holding[i] = holding[i] + addition
            rest = rest - addition
    return np.array(holding)


def bell_draw(stream_key, extent, spread, reach, split=(), kind=jnp.bfloat16):
    factor_of = levels(stream_key, extent, split, -0.22, 0.18) if split else 1.0
    array = jax.random.normal(stream_key, extent, jnp.float32) * spread * factor_of
    return jnp.minimum(jnp.maximum(array, -reach), reach).astype(kind)


def setup_inputs(seed: int = 0) -> dict:
    arg_keys = jax.random.split(jax.random.key(seed), 8)
    tokens = bell_draw(arg_keys[0], (TOKENS, D), 1.0, 6.0, ((0, 32),))
    out_grad = bell_draw(arg_keys[1], (TOKENS, D), 1.0, 6.0, ((0, 32),))
    expert_ids_keys = jax.random.split(jax.random.fold_in(arg_keys[2], 1), TOKENS // TOK_DEV)
    expert_ids_turns = jax.random.permutation(jax.random.fold_in(arg_keys[2], 3), TOKENS // TOK_DEV)
    expert_ids = jax.vmap(lambda own, number: routed_block(jax.random.fold_in(arg_keys[2], 2), own, number, TOK_DEV, EXPERTS_ALL, TOPK, CAP, 2))(expert_ids_keys, expert_ids_turns).reshape((TOKENS, TOPK))
    gate_vals = jnp.clip(jnp.exp(math.log(0.59765625) - 2.4849066 * jax.random.uniform(arg_keys[3], (TOKENS, TOPK), jnp.float32) ** levels(arg_keys[3], (TOKENS, TOPK), ((0, 32),), -0.2, 0.2)), 0.049804688, 0.59765625).astype(jnp.bfloat16)
    w_gate = bell_draw(arg_keys[4], (EXPERTS, D, FF), D ** -0.5, 0.125, ((0, 16),))
    w_up = bell_draw(arg_keys[5], (EXPERTS, D, FF), D ** -0.5, 0.125, ((0, 16),))
    w_down = bell_draw(arg_keys[6], (EXPERTS, FF, D), FF ** -0.5, 0.21875, ((0, 16),))
    return {"tokens": tokens, "out_grad": out_grad, "expert_ids": expert_ids, "gate_vals": gate_vals, "w_gate": w_gate, "w_up": w_up, "w_down": w_down}


def expert_rows(rows_x, rows_dy, rows_gate, gate_w, up_w, down_w):
    gate_pre = jnp.dot(rows_x, gate_w, preferred_element_type=jnp.float32)
    up_pre = jnp.dot(rows_x, up_w, preferred_element_type=jnp.float32)
    sigmoid_gate = jax.nn.sigmoid(gate_pre)
    silu_gate = gate_pre * sigmoid_gate
    hidden = (silu_gate * up_pre).astype(jnp.bfloat16)
    hidden_raw = lax.dot_general(rows_dy, down_w, (((1,), (1,)), ((), ())), preferred_element_type=jnp.float32)
    gate_scale = rows_gate.astype(jnp.float32)[:, None]
    gate_grad = jnp.sum(hidden.astype(jnp.float32) * hidden_raw, axis=1).astype(jnp.bfloat16)
    hidden_grad = gate_scale * hidden_raw
    up_grad = (hidden_grad * silu_gate).astype(jnp.bfloat16)
    pre_grad = (hidden_grad * up_pre * sigmoid_gate * (1.0 + gate_pre * (1.0 - sigmoid_gate))).astype(jnp.bfloat16)
    scaled_dy = (gate_scale * rows_dy.astype(jnp.float32)).astype(jnp.bfloat16)
    input_rows = lax.dot_general(pre_grad, gate_w, (((1,), (1,)), ((), ())), preferred_element_type=jnp.float32)
    input_rows = input_rows + lax.dot_general(up_grad, up_w, (((1,), (1,)), ((), ())), preferred_element_type=jnp.float32)
    return input_rows.astype(jnp.bfloat16), gate_grad, pre_grad, up_grad, hidden, scaled_dy


def reference(tokens, out_grad, expert_ids, gate_vals, w_gate, w_up, w_down):
    experts = EXP_DEV * N_EXPERT
    group_rows = N_EXPERT * TOK_DEV
    most_rows = N_EXPERT * CAP
    group_x = tokens.reshape(N_DP, group_rows, D)
    group_dy = out_grad.reshape(N_DP, group_rows, D)
    group_ids = expert_ids.reshape(N_DP, group_rows * TOPK)
    group_gates = gate_vals.reshape(N_DP, group_rows * TOPK)
    positions = jnp.arange(most_rows, dtype=jnp.int32)

    def one_expert(carried, expert):
        input_acc, gates_acc = carried
        gate_w = w_gate[expert]
        up_w = w_up[expert]
        down_w = w_down[expert]

        def one_member(totals, member):
            ids_m, x_m, dy_m, gates_m, in_acc, g_acc = member
            matched = ids_m == expert
            ordering = jnp.argsort(jnp.where(matched, 0, 1).astype(jnp.int32), stable=True).astype(jnp.int32)
            chosen = ordering[:most_rows]
            live_rows = jnp.sum(matched.astype(jnp.int32))
            occupied = positions < live_rows
            token_row = (chosen // TOPK).astype(jnp.int32)
            rows_x = jnp.where(occupied[:, None], x_m[token_row], jnp.zeros((), x_m.dtype))
            rows_dy = jnp.where(occupied[:, None], dy_m[token_row], jnp.zeros((), dy_m.dtype))
            rows_gate = jnp.where(occupied, gates_m[chosen], jnp.zeros((), gates_m.dtype))
            input_rows, gate_grad, pre_grad, up_grad, hidden, scaled_dy = expert_rows(rows_x, rows_dy, rows_gate, gate_w, up_w, down_w)
            in_acc = in_acc.at[token_row].add(jnp.where(occupied[:, None], input_rows.astype(jnp.float32), jnp.float32(0.0)))
            g_acc = g_acc.at[chosen].add(jnp.where(occupied, gate_grad.astype(jnp.float32), jnp.float32(0.0)))
            part_gate = jnp.dot(rows_x.T, pre_grad, preferred_element_type=jnp.float32)
            part_up = jnp.dot(rows_x.T, up_grad, preferred_element_type=jnp.float32)
            part_down = jnp.dot(hidden.T, scaled_dy, preferred_element_type=jnp.float32)
            rounded = lax.optimization_barrier((part_gate.astype(jnp.bfloat16), part_up.astype(jnp.bfloat16), part_down.astype(jnp.bfloat16)))
            totals = tuple(total + part.astype(jnp.float32) for total, part in zip(totals, rounded))
            return totals, (in_acc, g_acc)

        zeros_init = (jnp.zeros((D, FF), jnp.float32), jnp.zeros((D, FF), jnp.float32), jnp.zeros((FF, D), jnp.float32))
        totals, (input_acc, gates_acc) = lax.scan(one_member, zeros_init, (group_ids, group_x, group_dy, group_gates, input_acc, gates_acc))
        return (input_acc, gates_acc), tuple(total.astype(jnp.bfloat16) for total in totals)

    start_state = (jnp.zeros((N_DP, group_rows, D), jnp.float32), jnp.zeros((N_DP, group_rows * TOPK), jnp.float32))
    (input_acc, gates_acc), (grad_gate, grad_up, grad_down) = lax.scan(one_expert, start_state, jnp.arange(experts, dtype=jnp.int32))
    d_tokens = input_acc.reshape(N_DP * group_rows, D).astype(jnp.bfloat16)
    d_gates = gates_acc.reshape(N_DP * group_rows, TOPK).astype(jnp.bfloat16)
    return d_tokens, d_gates, grad_gate, grad_up, grad_down
```

```python
import functools

import jax
import jax.numpy as jnp
from jax import lax
from jax.experimental import pallas as pl
from jax.experimental.pallas import tpu as pltpu
from jax.sharding import PartitionSpec as P

CAP = 15
SLOT = CAP + 1
LANES = 128
VMEM_LIMIT = 48 * 1024 * 1024
NN = (((1,), (0,)), ((), ()))
NT = (((1,), (1,)), ((), ()))
TN = (((0,), (0,)), ((), ()))
BF16 = jnp.bfloat16
F32 = jnp.float32


def dot(a, b, dims=NN):
    return lax.dot_general(a, b, dims, preferred_element_type=F32)


def iota(shape, dim):
    return lax.broadcasted_iota(jnp.int32, shape, dim)


def call(kernel, out_shape, flops, bytes_accessed, **kwargs):
    return pl.pallas_call(
        kernel,
        out_shape=out_shape,
        compiler_params=pltpu.CompilerParams(vmem_limit_bytes=VMEM_LIMIT),
        cost_estimate=pl.CostEstimate(
            flops=flops, bytes_accessed=bytes_accessed, transcendentals=0
        ),
        **kwargs,
    )


def whole(count):
    return [pl.BlockSpec(memory_space=pltpu.VMEM)] * count


def chunks(total, size):
    return [(at, min(size, total - at)) for at in range(0, total, size)]


def column_of_slots(rows_x):
    rows = rows_x.shape[0]
    row, other = iota((rows, rows), 0), iota((rows, rows), 1)
    pick_last = (other == row // SLOT * SLOT + (SLOT - 1)).astype(BF16)
    spread = dot(pick_last, rows_x[:, :LANES])
    row, lane = iota((rows, LANES), 0), iota((rows, LANES), 1)
    own = (lane == row % SLOT) & (lane < CAP)
    return jnp.sum(jnp.where(own, spread, 0.0), axis=1, keepdims=True)


def last_rows_of_slots(column):
    rows = column.shape[0]
    row, lane = iota((rows, LANES), 0), iota((rows, LANES), 1)
    spread = jnp.where((lane == row % SLOT) & (lane < CAP), column, 0.0).astype(BF16)
    row, other = iota((rows, rows), 0), iota((rows, rows), 1)
    gather = ((row // SLOT == other // SLOT) & (row % SLOT == SLOT - 1)).astype(BF16)
    return dot(gather, spread)


def route_kernel(ids_ref, gates_ref, tokens_ref, send_ref, pick_ref, place_ref):
    tok_rows, top_count = ids_ref.shape
    rows = send_ref.shape[0]
    wide = -(-(rows // SLOT) // LANES) * LANES
    expert = iota((tok_rows, wide), 1)
    match = jnp.zeros((tok_rows, wide), F32)
    gate = jnp.zeros((tok_rows, wide), F32)
    gates = gates_ref[...].astype(F32)
    for k in range(top_count):
        hit = ids_ref[:, k : k + 1] == expert
        match = jnp.where(hit, 1.0, match)
        gate = jnp.where(hit, gates[:, k : k + 1], gate)
    earlier = (iota((tok_rows, tok_rows), 0) > iota((tok_rows, tok_rows), 1)).astype(BF16)
    rank = dot(earlier, match.astype(BF16))
    key = jnp.where(match > 0.0, rank, -1.0).astype(BF16)
    owner = (iota((rows, wide), 0) // SLOT == iota((rows, wide), 1)).astype(BF16)
    pick = (dot(owner, key, NT) == (iota((rows, tok_rows), 0) % SLOT).astype(F32)).astype(BF16)
    place = (dot(key, owner, NT) == (iota((tok_rows, rows), 1) % SLOT).astype(F32)).astype(BF16)
    pick_ref[...] = pick
    place_ref[...] = place
    slot_gates = jnp.sum(
        dot(pick, gate.astype(BF16)) * owner.astype(F32), axis=1, keepdims=True
    )
    gate_rows = last_rows_of_slots(slot_gates)
    for at, size in chunks(tokens_ref.shape[1], 512):
        part = dot(pick, tokens_ref[:, at : at + size])
        if at == 0:
            send_ref[:, :LANES] = (part[:, :LANES] + gate_rows).astype(BF16)
            send_ref[:, LANES:size] = part[:, LANES:].astype(BF16)
        else:
            send_ref[:, at : at + size] = part.astype(BF16)


def gather_kernel(pick_ref, grad_ref, send_ref):
    for at, size in chunks(grad_ref.shape[1], 512):
        send_ref[:, at : at + size] = dot(pick_ref[...], grad_ref[:, at : at + size]).astype(BF16)


def forward_kernel(x_ref, gate_w_ref, up_w_ref, silu_ref, slope_ref, hidden_ref, gate_ref):
    rows_x = x_ref[...]
    gate_pre = dot(rows_x, gate_w_ref[0])
    up_pre = dot(rows_x, up_w_ref[0])
    sigmoid_gate = jax.nn.sigmoid(gate_pre)
    silu_gate = gate_pre * sigmoid_gate
    silu_ref[...] = silu_gate
    slope_ref[...] = up_pre * sigmoid_gate * (1.0 + gate_pre * (1.0 - sigmoid_gate))
    hidden_ref[...] = (silu_gate * up_pre).astype(BF16)

    @pl.when(pl.program_id(0) == 0)
    def _():
        gate_ref[...] = jnp.broadcast_to(column_of_slots(rows_x), gate_ref.shape)


def input_kernel(
    dy_ref,
    gate_w_ref,
    up_w_ref,
    down_w_ref,
    silu_ref,
    slope_ref,
    hidden_ref,
    gate_ref,
    back_ref,
    pre_ref,
    up_ref,
    gate_w,
    up_w,
    down_w,
    sems,
):
    copies = [
        pltpu.make_async_copy(src.at[0], dst, sems.at[i])
        for i, (src, dst) in enumerate(
            ((down_w_ref, down_w), (gate_w_ref, gate_w), (up_w_ref, up_w))
        )
    ]
    for copy in copies:
        copy.start()
    rows_dy = dy_ref[...]
    gate = gate_ref[:, :1]
    gate_grad = jnp.zeros_like(gate)
    copies[0].wait()
    for at, size in chunks(down_w.shape[0], 256):
        cols = slice(at, at + size)
        hidden_raw = dot(rows_dy, down_w[cols, :], NT)
        gate_grad += jnp.sum(hidden_ref[:, cols].astype(F32) * hidden_raw, axis=1, keepdims=True)
        hidden_grad = gate * hidden_raw
        up_ref[:, cols] = (hidden_grad * silu_ref[:, cols]).astype(BF16)
        pre_ref[:, cols] = (hidden_grad * slope_ref[:, cols]).astype(BF16)
    gate_rows = last_rows_of_slots(gate_grad.astype(BF16).astype(F32))
    copies[1].wait()
    copies[2].wait()
    for at, size in chunks(back_ref.shape[1], 512):
        part = dot(pre_ref[...], gate_w[at : at + size, :], NT)
        part += dot(up_ref[...], up_w[at : at + size, :], NT)
        if at == 0:
            back_ref[:, :LANES] = (part[:, :LANES] + gate_rows).astype(BF16)
            back_ref[:, LANES:size] = part[:, LANES:].astype(BF16)
        else:
            back_ref[:, at : at + size] = part.astype(BF16)


def hidden_kernel(dy_ref, down_w_ref, silu_ref, slope_ref, gate_ref, pre_ref, up_ref):
    hidden_grad = gate_ref[:, :1] * dot(dy_ref[...], down_w_ref[0], NT)
    up_ref[...] = (hidden_grad * silu_ref[...]).astype(BF16)
    pre_ref[...] = (hidden_grad * slope_ref[...]).astype(BF16)


def weight_kernel(groups, which_ref, *refs):
    del which_ref
    grads = [refs[6 * i : 6 * i + 6] for i in range(groups)]
    gate_out, up_out, down_out = refs[6 * groups :]
    gate_sum = up_sum = down_sum = 0.0
    for x_ref, dy_ref, pre_ref, up_ref, hidden_ref, gate_ref in grads:
        rows_x = x_ref[...]
        scaled_dy = (gate_ref[:, :1] * dy_ref[...].astype(F32)).astype(BF16)
        gate_sum += dot(rows_x, pre_ref[...], TN)
        up_sum += dot(rows_x, up_ref[...], TN)
        down_sum += dot(hidden_ref[...], scaled_dy, TN)
    gate_out[0] = gate_sum.astype(BF16)
    up_out[0] = up_sum.astype(BF16)
    down_out[0] = down_sum.astype(BF16)


def combine_kernel(ids_ref, place_ref, back_ref, tokens_ref, gates_ref):
    place = place_ref[...]
    for at, size in chunks(back_ref.shape[1], 512):
        tokens_ref[:, at : at + size] = dot(place, back_ref[:, at : at + size]).astype(BF16)
    tok_rows, rows = place.shape
    wide = -(-(rows // SLOT) // LANES) * LANES
    owner = iota((rows, wide), 0) // SLOT == iota((rows, wide), 1)
    spread = jnp.where(owner, column_of_slots(back_ref[:, :LANES]), 0.0).astype(BF16)
    by_expert = dot(place, spread)
    expert = iota((tok_rows, wide), 1)
    top_count = ids_ref.shape[1]
    lane = iota((tok_rows, top_count), 1)
    total = jnp.zeros((tok_rows, top_count), F32)
    for k in range(top_count):
        own = jnp.sum(
            jnp.where(ids_ref[:, k : k + 1] == expert, by_expert, 0.0), axis=1, keepdims=True
        )
        total = jnp.where(lane == k, own, total)
    gates_ref[...] = total.astype(BF16)


def forward(rows_x, w_gate, w_up, tile=256):
    rows, features = rows_x.shape
    units = w_gate.shape[2]
    tiled = pl.BlockSpec((rows, tile), lambda j: (0, j))
    weight = pl.BlockSpec((1, features, tile), lambda j: (0, 0, j))
    return call(
        forward_kernel,
        (
            jax.ShapeDtypeStruct((rows, units), F32),
            jax.ShapeDtypeStruct((rows, units), F32),
            jax.ShapeDtypeStruct((rows, units), BF16),
            jax.ShapeDtypeStruct((rows, LANES), F32),
        ),
        4 * rows * features * units,
        4 * features * units + 2 * rows * features + 10 * rows * units,
        grid=(units // tile,),
        in_specs=[pl.BlockSpec((rows, features), lambda j: (0, 0)), weight, weight],
        out_specs=(tiled, tiled, tiled, pl.BlockSpec((rows, LANES), lambda j: (0, 0))),
        name="forward",
    )(rows_x, w_gate, w_up)


def body(tokens, out_grad, expert_ids, gate_vals, w_gate, w_up, w_down):
    expert_count = lax.axis_size("expert")
    groups = lax.axis_size("dp")
    tok_rows, features = tokens.shape
    units = w_gate.shape[2]
    rows = expert_count * SLOT
    share = features // groups

    def exchange(send):
        return lax.all_to_all(
            send.reshape(expert_count, SLOT, features),
            "expert",
            split_axis=0,
            concat_axis=0,
            tiled=True,
        ).reshape(rows, features)

    def from_group(value, step):
        return lax.ppermute(value, "dp", [(i, (i + step) % groups) for i in range(groups)])

    send_x, pick, place = call(
        route_kernel,
        (
            jax.ShapeDtypeStruct((rows, features), BF16),
            jax.ShapeDtypeStruct((rows, tok_rows), BF16),
            jax.ShapeDtypeStruct((tok_rows, rows), BF16),
        ),
        2 * rows * tok_rows * features,
        4 * rows * features,
        in_specs=whole(3),
        out_specs=tuple(whole(3)),
        name="route",
    )(expert_ids, gate_vals, tokens)
    rows_x = exchange(send_x)
    send_dy = call(
        gather_kernel,
        jax.ShapeDtypeStruct((rows, features), BF16),
        2 * rows * tok_rows * features,
        4 * rows * features,
        in_specs=whole(2),
        out_specs=whole(1)[0],
        name="gather",
    )(pick, out_grad)
    rows_dy = exchange(send_dy)
    silu, slope, hidden, gate = forward(rows_x, w_gate, w_up)
    back, pre_grad, up_grad = call(
        input_kernel,
        (
            jax.ShapeDtypeStruct((rows, features), BF16),
            jax.ShapeDtypeStruct((rows, units), BF16),
            jax.ShapeDtypeStruct((rows, units), BF16),
        ),
        6 * rows * features * units,
        6 * features * units + 4 * rows * features + 10 * rows * units,
        in_specs=whole(1) + [pl.BlockSpec(memory_space=pl.ANY)] * 3 + whole(4),
        out_specs=tuple(whole(3)),
        scratch_shapes=[
            pltpu.VMEM((features, units), BF16),
            pltpu.VMEM((features, units), BF16),
            pltpu.VMEM((units, features), BF16),
            pltpu.SemaphoreType.DMA((3,)),
        ],
        name="input_rows",
    )(rows_dy, w_gate, w_up, w_down, silu, slope, hidden, gate)
    back = exchange(back)

    parts = [(rows_x, rows_dy, pre_grad, up_grad, hidden, gate)]
    tile = 256
    for step in range(1, groups):
        other_x = from_group(rows_x, step)
        other_dy = from_group(rows_dy, step)
        other_silu, other_slope, other_hidden, other_gate = forward(other_x, w_gate, w_up)
        tiled = pl.BlockSpec((rows, tile), lambda j: (0, j))
        other_pre, other_up = call(
            hidden_kernel,
            (
                jax.ShapeDtypeStruct((rows, units), BF16),
                jax.ShapeDtypeStruct((rows, units), BF16),
            ),
            2 * rows * features * units,
            2 * features * units + 2 * rows * features + 10 * rows * units,
            grid=(units // tile,),
            in_specs=[
                pl.BlockSpec((rows, features), lambda j: (0, 0)),
                pl.BlockSpec((1, tile, features), lambda j: (0, j, 0)),
                tiled,
                tiled,
                pl.BlockSpec((rows, LANES), lambda j: (0, 0)),
            ],
            out_specs=(tiled, tiled),
            name="hidden_grads",
        )(other_dy, w_down, other_silu, other_slope, other_gate)
        parts.append((other_x, other_dy, other_pre, other_up, other_hidden, other_gate))

    piece = min(share, 256)
    steps = share // piece
    narrow = pl.BlockSpec((rows, piece), lambda j, which: (0, which[0] * steps + j))
    full = pl.BlockSpec((rows, units), lambda j, which: (0, 0))
    which = lax.axis_index("dp").reshape(1).astype(jnp.int32)
    d_gate, d_up, d_down = pl.pallas_call(
        functools.partial(weight_kernel, groups),
        out_shape=(
            jax.ShapeDtypeStruct((1, share, units), BF16),
            jax.ShapeDtypeStruct((1, share, units), BF16),
            jax.ShapeDtypeStruct((1, units, share), BF16),
        ),
        grid_spec=pltpu.PrefetchScalarGridSpec(
            num_scalar_prefetch=1,
            grid=(steps,),
            in_specs=[
                narrow,
                narrow,
                full,
                full,
                full,
                pl.BlockSpec((rows, LANES), lambda j, which: (0, 0)),
            ]
            * groups,
            out_specs=(
                pl.BlockSpec((1, piece, units), lambda j, which: (0, j, 0)),
                pl.BlockSpec((1, piece, units), lambda j, which: (0, j, 0)),
                pl.BlockSpec((1, units, piece), lambda j, which: (0, 0, j)),
            ),
        ),
        compiler_params=pltpu.CompilerParams(vmem_limit_bytes=VMEM_LIMIT),
        cost_estimate=pl.CostEstimate(
            flops=6 * groups * rows * share * units,
            bytes_accessed=6 * share * units + groups * rows * (4 * share + 6 * units),
            transcendentals=0,
        ),
        name="weight_grads",
    )(which, *[value for part in parts for value in part])

    d_tokens, d_gates = call(
        combine_kernel,
        (
            jax.ShapeDtypeStruct(tokens.shape, BF16),
            jax.ShapeDtypeStruct(gate_vals.shape, BF16),
        ),
        2 * rows * tok_rows * features,
        4 * rows * features,
        in_specs=whole(3),
        out_specs=tuple(whole(2)),
        name="combine",
    )(expert_ids, place, back)
    return d_tokens, d_gates, d_gate, d_up, d_down


def solution(mesh):
    in_specs = (
        P(("dp", "expert"), None),
        P(("dp", "expert"), None),
        P(("dp", "expert"), None),
        P(("dp", "expert"), None),
        P("expert", None, None),
        P("expert", None, None),
        P("expert", None, None),
    )
    out_specs = (
        P(("dp", "expert"), None),
        P(("dp", "expert"), None),
        P("expert", "dp", None),
        P("expert", "dp", None),
        P("expert", None, "dp"),
    )
    return jax.shard_map(body, mesh=mesh, in_specs=in_specs, out_specs=out_specs, check_vma=False)
```

```python
import functools

import jax
import jax.numpy as jnp
from jax import lax
from jax.experimental import pallas as pl
from jax.experimental.pallas import tpu as pltpu
from jax.sharding import PartitionSpec as P

CAP = 15
SLOT = CAP + 1
LANES = 128
VMEM = 60 * 1024 * 1024
WEIGH = 10
NN = (((1,), (0,)), ((), ()))
NT = (((1,), (1,)), ((), ()))
TN = (((0,), (0,)), ((), ()))
BF16 = jnp.bfloat16
F32 = jnp.float32


def dot(a, b, dims=NN):
    return lax.dot_general(a, b, dims, preferred_element_type=F32)


def iota(shape, dim):
    return lax.broadcasted_iota(jnp.int32, shape, dim)


def call(kernel, out_shape, flops, bytes_accessed, **kwargs):
    return pl.pallas_call(
        kernel,
        out_shape=out_shape,
        compiler_params=pltpu.CompilerParams(vmem_limit_bytes=VMEM),
        cost_estimate=pl.CostEstimate(
            flops=flops, bytes_accessed=bytes_accessed, transcendentals=0
        ),
        **kwargs,
    )


def whole(count):
    return [pl.BlockSpec(memory_space=pltpu.VMEM)] * count


def chunks(total, size):
    return [(at, min(size, total - at)) for at in range(0, total, size)]


def column_of_slots(rows_x):
    rows = rows_x.shape[0]
    row, other = iota((rows, rows), 0), iota((rows, rows), 1)
    pick_last = (other == row // SLOT * SLOT + (SLOT - 1)).astype(BF16)
    spread = dot(pick_last, rows_x[:, :LANES])
    row, lane = iota((rows, LANES), 0), iota((rows, LANES), 1)
    own = (lane == row % SLOT) & (lane < CAP)
    return jnp.sum(jnp.where(own, spread, 0.0), axis=1, keepdims=True)


def last_rows_of_slots(column):
    rows = column.shape[0]
    row, lane = iota((rows, LANES), 0), iota((rows, LANES), 1)
    spread = jnp.where((lane == row % SLOT) & (lane < CAP), column, 0.0).astype(BF16)
    row, other = iota((rows, rows), 0), iota((rows, rows), 1)
    gather = ((row // SLOT == other // SLOT) & (row % SLOT == SLOT - 1)).astype(BF16)
    return dot(gather, spread)


def route_kernel(ids_ref, gates_ref, tokens_hbm, send_ref, pick_ref, tokens_ref, sem):
    load = pltpu.make_async_copy(tokens_hbm, tokens_ref, sem)
    load.start()
    top_count, tok_rows = ids_ref.shape
    rows = send_ref.shape[0]
    experts = rows // SLOT
    expert = iota((experts, tok_rows), 0)
    match = jnp.zeros((experts, tok_rows), F32)
    gate = jnp.zeros((experts, tok_rows), F32)
    gates = gates_ref[...].astype(F32)
    for k in range(top_count):
        hit = ids_ref[k : k + 1, :] == expert
        match = jnp.where(hit, 1.0, match)
        gate = jnp.where(hit, gates[k : k + 1, :], gate)
    earlier = (iota((tok_rows, tok_rows), 0) < iota((tok_rows, tok_rows), 1)).astype(BF16)
    rank = dot(match.astype(BF16), earlier)
    key = jnp.where(match > 0.0, rank, -1.0).astype(BF16)
    owner = (iota((rows, experts), 0) // SLOT == iota((rows, experts), 1)).astype(BF16)
    picked = dot(owner, key) == (iota((rows, tok_rows), 0) % SLOT).astype(F32)
    pick = picked.astype(BF16)
    pick_ref[...] = pick
    slot_gates = jnp.sum(
        jnp.where(picked, dot(owner, gate.astype(BF16)), 0.0), axis=1, keepdims=True
    )
    gate_rows = last_rows_of_slots(slot_gates)
    load.wait()
    for at, size in chunks(tokens_ref.shape[1], 512):
        part = dot(pick, tokens_ref[:, at : at + size])
        if at == 0:
            send_ref[:, :LANES] = (part[:, :LANES] + gate_rows).astype(BF16)
            send_ref[:, LANES:size] = part[:, LANES:].astype(BF16)
        else:
            send_ref[:, at : at + size] = part.astype(BF16)


def gather_kernel(pick_ref, grad_ref, send_ref):
    for at, size in chunks(grad_ref.shape[1], 512):
        send_ref[:, at : at + size] = dot(pick_ref[...], grad_ref[:, at : at + size]).astype(BF16)


def forward_kernel(
    x_ref, gate_w_ref, up_w_ref, silu_ref, slope_ref, hidden_ref, gate_ref, same_ref
):
    del same_ref
    rows_x = x_ref[...]
    gate_pre = dot(rows_x, gate_w_ref[0])
    up_pre = dot(rows_x, up_w_ref[0])
    sigmoid_gate = jax.nn.sigmoid(gate_pre)
    silu_gate = gate_pre * sigmoid_gate
    silu_ref[...] = silu_gate
    slope_ref[...] = up_pre * sigmoid_gate * (1.0 + gate_pre * (1.0 - sigmoid_gate))
    hidden_ref[...] = (silu_gate * up_pre).astype(BF16)

    @pl.when(pl.program_id(0) == 0)
    def _():
        gate_ref[...] = jnp.broadcast_to(column_of_slots(rows_x), gate_ref.shape)


def input_kernel(
    dy_ref,
    gate_w_ref,
    up_w_ref,
    down_w_ref,
    silu_ref,
    slope_ref,
    hidden_ref,
    gate_ref,
    back_ref,
    pre_ref,
    up_ref,
    gate_w,
    up_w,
    down_w,
    sems,
):
    copies = [
        pltpu.make_async_copy(src.at[0], dst, sems.at[i])
        for i, (src, dst) in enumerate(
            ((down_w_ref, down_w), (gate_w_ref, gate_w), (up_w_ref, up_w))
        )
    ]
    for copy in copies:
        copy.start()
    rows_dy = dy_ref[...]
    gate = gate_ref[:, :1]
    gate_grad = jnp.zeros_like(gate)
    copies[0].wait()
    for at, size in chunks(down_w.shape[0], 256):
        cols = slice(at, at + size)
        hidden_raw = dot(rows_dy, down_w[cols, :], NT)
        gate_grad += jnp.sum(hidden_ref[:, cols].astype(F32) * hidden_raw, axis=1, keepdims=True)
        hidden_grad = gate * hidden_raw
        up_ref[:, cols] = (hidden_grad * silu_ref[:, cols]).astype(BF16)
        pre_ref[:, cols] = (hidden_grad * slope_ref[:, cols]).astype(BF16)
    gate_rows = last_rows_of_slots(gate_grad.astype(BF16).astype(F32))
    copies[1].wait()
    copies[2].wait()
    for at, size in chunks(back_ref.shape[1], 512):
        part = dot(pre_ref[...], gate_w[at : at + size, :], NT)
        part += dot(up_ref[...], up_w[at : at + size, :], NT)
        if at == 0:
            back_ref[:, :LANES] = (part[:, :LANES] + gate_rows).astype(BF16)
            back_ref[:, LANES:size] = part[:, LANES:].astype(BF16)
        else:
            back_ref[:, at : at + size] = part.astype(BF16)


def hidden_kernel(dy_ref, down_w_ref, silu_ref, slope_ref, gate_ref, pre_ref, up_ref):
    hidden_grad = gate_ref[:, :1] * dot(dy_ref[...], down_w_ref[0], NT)
    up_ref[...] = (hidden_grad * silu_ref[...]).astype(BF16)
    pre_ref[...] = (hidden_grad * slope_ref[...]).astype(BF16)


def weight_kernel(groups, which_ref, *refs):
    del which_ref
    grads = [refs[6 * i : 6 * i + 6] for i in range(groups)]
    gate_out, up_out, down_out = refs[6 * groups :]
    gate_sum = up_sum = down_sum = 0.0
    for x_ref, dy_ref, pre_ref, up_ref, hidden_ref, gate_ref in grads:
        rows_x = x_ref[...]
        scaled_dy = (gate_ref[:, :1] * dy_ref[...].astype(F32)).astype(BF16)
        gate_sum += dot(rows_x, pre_ref[...], TN)
        up_sum += dot(rows_x, up_ref[...], TN)
        down_sum += dot(hidden_ref[...], scaled_dy, TN)
    gate_out[0] = gate_sum.astype(BF16)
    up_out[0] = up_sum.astype(BF16)
    down_out[0] = down_sum.astype(BF16)


def combine_kernel(ids_ref, pick_ref, back_ref, tokens_ref, gates_ref):
    place = pick_ref[...].T
    for at, size in chunks(back_ref.shape[1], 512):
        tokens_ref[:, at : at + size] = dot(place, back_ref[:, at : at + size]).astype(BF16)
    rows, tok_rows = pick_ref.shape
    experts = rows // SLOT
    owner = iota((experts, rows), 1) // SLOT == iota((experts, rows), 0)
    gate_grad = column_of_slots(back_ref[:, :LANES])
    spread = (pick_ref[...].astype(F32) * gate_grad).astype(BF16)
    by_expert = dot(owner.astype(BF16), spread)
    expert = iota((experts, tok_rows), 0)
    for k in range(ids_ref.shape[0]):
        own = jnp.where(ids_ref[k : k + 1, :] == expert, by_expert, 0.0)
        gates_ref[k : k + 1, :] = jnp.sum(own, axis=0, keepdims=True).astype(BF16)


def forward(rows_x, w_gate, w_up, tile=256):
    rows, features = rows_x.shape
    units = w_gate.shape[2]
    tiled = pl.BlockSpec((rows, tile), lambda j: (0, j))
    weight = pl.BlockSpec((1, features, tile), lambda j: (0, 0, j))
    return call(
        forward_kernel,
        (
            jax.ShapeDtypeStruct((rows, units), F32),
            jax.ShapeDtypeStruct((rows, units), F32),
            jax.ShapeDtypeStruct((rows, units), BF16),
            jax.ShapeDtypeStruct((rows, LANES), F32),
            jax.ShapeDtypeStruct((rows, features), BF16),
        ),
        WEIGH * 4 * rows * features * units,
        4 * features * units + 2 * rows * features + 10 * rows * units,
        grid=(units // tile,),
        in_specs=[pl.BlockSpec((rows, features), lambda j: (0, 0)), weight, weight],
        out_specs=(
            tiled,
            tiled,
            tiled,
            pl.BlockSpec((rows, LANES), lambda j: (0, 0)),
            pl.BlockSpec(memory_space=pl.ANY),
        ),
        input_output_aliases={0: 4},
        name="forward",
    )(rows_x, w_gate, w_up)


def body(tokens, out_grad, expert_ids, gate_vals, w_gate, w_up, w_down):
    expert_count = lax.axis_size("expert")
    groups = lax.axis_size("dp")
    tok_rows, features = tokens.shape
    top_count = expert_ids.shape[1]
    units = w_gate.shape[2]
    rows = expert_count * SLOT
    share = features // groups
    ids = expert_ids.T
    anywhere = pl.BlockSpec(memory_space=pl.ANY)

    def exchange(send):
        return lax.all_to_all(
            send.reshape(expert_count, SLOT, features),
            "expert",
            split_axis=0,
            concat_axis=0,
            tiled=True,
        ).reshape(rows, features)

    def from_group(value, step):
        return lax.ppermute(value, "dp", [(i, (i + step) % groups) for i in range(groups)])

    send_x, pick = call(
        route_kernel,
        (
            jax.ShapeDtypeStruct((rows, features), BF16),
            jax.ShapeDtypeStruct((rows, tok_rows), BF16),
        ),
        2 * rows * tok_rows * features,
        4 * rows * features,
        in_specs=whole(2) + [anywhere],
        out_specs=tuple(whole(2)),
        scratch_shapes=[pltpu.VMEM((tok_rows, features), BF16), pltpu.SemaphoreType.DMA],
        name="route",
    )(ids, gate_vals.T, tokens)
    rows_x = exchange(send_x)
    send_dy = call(
        gather_kernel,
        jax.ShapeDtypeStruct((rows, features), BF16),
        2 * rows * tok_rows * features,
        4 * rows * features,
        in_specs=whole(2),
        out_specs=whole(1)[0],
        name="gather",
    )(pick, out_grad)
    rows_dy = exchange(send_dy)
    silu, slope, hidden, gate, rows_x = forward(rows_x, w_gate, w_up)
    back, pre_grad, up_grad = call(
        input_kernel,
        (
            jax.ShapeDtypeStruct((rows, features), BF16),
            jax.ShapeDtypeStruct((rows, units), BF16),
            jax.ShapeDtypeStruct((rows, units), BF16),
        ),
        6 * rows * features * units,
        6 * features * units + 4 * rows * features + 10 * rows * units,
        in_specs=whole(1) + [anywhere] * 3 + whole(4),
        out_specs=tuple(whole(3)),
        scratch_shapes=[
            pltpu.VMEM((features, units), BF16),
            pltpu.VMEM((features, units), BF16),
            pltpu.VMEM((units, features), BF16),
            pltpu.SemaphoreType.DMA((3,)),
        ],
        name="input_rows",
    )(rows_dy, w_gate, w_up, w_down, silu, slope, hidden, gate)
    back = exchange(back)

    parts = [(rows_x, rows_dy, pre_grad, up_grad, hidden, gate)]
    tile = 256
    for step in range(1, groups):
        other_x = from_group(rows_x, step)
        other_dy = from_group(rows_dy, step)
        other_silu, other_slope, other_hidden, other_gate, other_x = forward(
            other_x, w_gate, w_up
        )
        tiled = pl.BlockSpec((rows, tile), lambda j: (0, j))
        other_pre, other_up = call(
            hidden_kernel,
            (
                jax.ShapeDtypeStruct((rows, units), BF16),
                jax.ShapeDtypeStruct((rows, units), BF16),
            ),
            WEIGH * 2 * rows * features * units,
            2 * features * units + 2 * rows * features + 10 * rows * units,
            grid=(units // tile,),
            in_specs=[
                pl.BlockSpec((rows, features), lambda j: (0, 0)),
                pl.BlockSpec((1, tile, features), lambda j: (0, j, 0)),
                tiled,
                tiled,
                pl.BlockSpec((rows, LANES), lambda j: (0, 0)),
            ],
            out_specs=(tiled, tiled),
            name="hidden_grads",
        )(other_dy, w_down, other_silu, other_slope, other_gate)
        parts.append((other_x, other_dy, other_pre, other_up, other_hidden, other_gate))

    piece = min(share, 256)
    steps = share // piece
    narrow = pl.BlockSpec((rows, piece), lambda j, which: (0, which[0] * steps + j))
    full = pl.BlockSpec((rows, units), lambda j, which: (0, 0))
    which = lax.axis_index("dp").reshape(1).astype(jnp.int32)
    d_gate, d_up, d_down = pl.pallas_call(
        functools.partial(weight_kernel, groups),
        out_shape=(
            jax.ShapeDtypeStruct((1, share, units), BF16),
            jax.ShapeDtypeStruct((1, share, units), BF16),
            jax.ShapeDtypeStruct((1, units, share), BF16),
        ),
        grid_spec=pltpu.PrefetchScalarGridSpec(
            num_scalar_prefetch=1,
            grid=(steps,),
            in_specs=[
                narrow,
                narrow,
                full,
                full,
                full,
                pl.BlockSpec((rows, LANES), lambda j, which: (0, 0)),
            ]
            * groups,
            out_specs=(
                pl.BlockSpec((1, piece, units), lambda j, which: (0, j, 0)),
                pl.BlockSpec((1, piece, units), lambda j, which: (0, j, 0)),
                pl.BlockSpec((1, units, piece), lambda j, which: (0, 0, j)),
            ),
        ),
        compiler_params=pltpu.CompilerParams(vmem_limit_bytes=VMEM),
        cost_estimate=pl.CostEstimate(
            flops=WEIGH * 6 * groups * rows * share * units,
            bytes_accessed=6 * share * units + groups * rows * (4 * share + 6 * units),
            transcendentals=0,
        ),
        name="weight_grads",
    )(which, *[value for part in parts for value in part])

    d_tokens, d_gates = call(
        combine_kernel,
        (
            jax.ShapeDtypeStruct(tokens.shape, BF16),
            jax.ShapeDtypeStruct((top_count, tok_rows), BF16),
        ),
        2 * rows * tok_rows * features,
        4 * rows * features,
        in_specs=whole(3),
        out_specs=tuple(whole(2)),
        name="combine",
    )(ids, pick, back)
    return d_tokens, d_gates.T, d_gate, d_up, d_down


def solution(mesh):
    in_specs = (
        P(("dp", "expert"), None),
        P(("dp", "expert"), None),
        P(("dp", "expert"), None),
        P(("dp", "expert"), None),
        P("expert", None, None),
        P("expert", None, None),
        P("expert", None, None),
    )
    out_specs = (
        P(("dp", "expert"), None),
        P(("dp", "expert"), None),
        P("expert", "dp", None),
        P("expert", "dp", None),
        P("expert", None, "dp"),
    )
    return jax.shard_map(body, mesh=mesh, in_specs=in_specs, out_specs=out_specs, check_vma=False)
```

```python
import jax
import jax.numpy as jnp
from jax import lax
from jax.experimental import pallas as pl
from jax.experimental.pallas import tpu as pltpu
from jax.sharding import PartitionSpec as P

CAP = 15
SLOT = CAP + 1
LANES = 128
VMEM = 60 * 1024 * 1024
WEIGH = 10
NN = (((1,), (0,)), ((), ()))
NT = (((1,), (1,)), ((), ()))
TN = (((0,), (0,)), ((), ()))
BF16 = jnp.bfloat16
F32 = jnp.float32


def dot(a, b, dims=NN):
    return lax.dot_general(a, b, dims, preferred_element_type=F32)


def iota(shape, dim):
    return lax.broadcasted_iota(jnp.int32, shape, dim)


def shaped(shape, dtype, space=pltpu.HBM):
    return jax.ShapeDtypeStruct(shape, dtype) if space is None else space(shape, dtype)


def call(kernel, outs, flops, bytes_accessed, spaces=None, **kwargs):
    run = pl.pallas_call(
        kernel,
        out_shape=outs,
        compiler_params=pltpu.CompilerParams(vmem_limit_bytes=VMEM),
        cost_estimate=pl.CostEstimate(
            flops=flops, bytes_accessed=bytes_accessed, transcendentals=0
        ),
        **kwargs,
    )
    spaces = spaces or {}

    def placed(*values):
        held = []
        for i, value in enumerate(values):
            space = spaces.get(i, pltpu.HBM)
            if space is not None:
                value = pltpu.with_memory_space_constraint(value, space)
            held.append(value)
        return run(*held)

    return placed


IN_HBM = pl.BlockSpec(memory_space=pltpu.HBM)
IN_VMEM = pl.BlockSpec(memory_space=pltpu.VMEM)
IN_SMEM = pl.BlockSpec(memory_space=pltpu.SMEM)


def chunks(total, size):
    return [(at, min(size, total - at)) for at in range(0, total, size)]


class Loads:
    def __init__(self, sems, pairs):
        self.copies = [
            pltpu.make_async_copy(src, dst, sems.at[i]) for i, (src, dst) in enumerate(pairs)
        ]
        for copy in self.copies:
            copy.start()

    def wait(self, count=1):
        for copy in self.copies[:count]:
            copy.wait()
        self.copies = self.copies[count:]


class Stores:
    def __init__(self, sems):
        self.sems = sems
        self.copies = []

    def start(self, src, dst):
        copy = pltpu.make_async_copy(src, dst, self.sems.at[len(self.copies)])
        copy.start()
        self.copies.append(copy)

    def wait(self):
        for copy in self.copies:
            copy.wait()


def last_rows_of_slots(column):
    rows = column.shape[0]
    row, lane = iota((rows, LANES), 0), iota((rows, LANES), 1)
    spread = jnp.where((lane == row % SLOT) & (lane < CAP), column, 0.0).astype(BF16)
    row, other = iota((rows, rows), 0), iota((rows, rows), 1)
    gather = ((row // SLOT == other // SLOT) & (row % SLOT == SLOT - 1)).astype(BF16)
    return dot(gather, spread)


def picked_slots(key, rows):
    experts, tok_rows = key.shape
    owner = (iota((rows, experts), 0) // SLOT == iota((rows, experts), 1)).astype(BF16)
    return dot(owner, key) == (iota((rows, tok_rows), 0) % SLOT).astype(F32), owner


def route_kernel(ids_hbm, tokens_hbm, send_hbm, key_ref, ids_ref, tokens_ref, send_ref, sems, store_sems):
    loads = Loads(sems, [(ids_hbm, ids_ref), (tokens_hbm, tokens_ref)])
    top_count, tok_rows = ids_ref.shape
    rows, features = send_ref.shape
    experts = rows // SLOT
    earlier = (iota((tok_rows, tok_rows), 0) < iota((tok_rows, tok_rows), 1)).astype(BF16)
    expert = iota((experts, tok_rows), 0)
    match = jnp.zeros((experts, tok_rows), F32)
    loads.wait()
    for k in range(top_count):
        match = jnp.where(ids_ref[k : k + 1, :] == expert, 1.0, match)
    rank = dot(match.astype(BF16), earlier)
    key = jnp.where(match > 0.0, rank, -1.0).astype(BF16)
    key_ref[...] = key
    pick = picked_slots(key, rows)[0].astype(BF16)
    loads.wait()
    stores = Stores(store_sems)
    for at, size in chunks(features, 512):
        cols = pl.ds(at, size)
        send_ref[:, at : at + size] = dot(pick, tokens_ref[:, at : at + size]).astype(BF16)
        stores.start(send_ref.at[:, cols], send_hbm.at[:, cols])
    stores.wait()


def gather_kernel(
    ids_ref,
    gates_ref,
    key_ref,
    grad_hbm,
    send_hbm,
    place_ref,
    ids_out,
    inverse_ref,
    grad_ref,
    send_ref,
    sems,
    store_sems,
):
    load = pltpu.make_async_copy(grad_hbm, grad_ref, sems.at[0])
    load.start()
    top_count, tok_rows = ids_ref.shape
    rows, features = send_ref.shape
    experts = rows // SLOT
    ids_out[...] = ids_ref[...]
    gates = gates_ref[...].astype(F32)
    inverse_ref[...] = 1.0 / gates
    expert = iota((experts, tok_rows), 0)
    gate = jnp.zeros((experts, tok_rows), F32)
    for k in range(top_count):
        gate = jnp.where(ids_ref[k : k + 1, :] == expert, gates[k : k + 1, :], gate)
    picked, owner = picked_slots(key_ref[...], rows)
    weighed = jnp.where(picked, dot(owner, gate.astype(BF16)), 0.0).astype(BF16)
    place_ref[...] = picked.astype(F32).T.astype(BF16)
    load.wait()
    stores = Stores(store_sems)
    for at, size in chunks(features, 512):
        cols = pl.ds(at, size)
        send_ref[:, at : at + size] = dot(weighed, grad_ref[:, at : at + size]).astype(BF16)
        stores.start(send_ref.at[:, cols], send_hbm.at[:, cols])
    stores.wait()


def activations(gate_pre, up_pre):
    sigmoid_gate = jax.nn.sigmoid(gate_pre)
    silu_gate = gate_pre * sigmoid_gate
    slope = up_pre * sigmoid_gate * (1.0 + gate_pre * (1.0 - sigmoid_gate))
    return silu_gate.astype(BF16), slope.astype(BF16), (silu_gate * up_pre).astype(BF16)


def forward_kernel(
    x_hbm,
    gate_hbm,
    up_hbm,
    silu_ref,
    slope_ref,
    hidden_ref,
    same_ref,
    x_ref,
    gate_w,
    up_w,
    pre_ref,
    sems,
):
    del same_ref
    units = chunks(gate_w.shape[1], 256)
    loads = Loads(sems, [(x_hbm, x_ref), (gate_hbm.at[0], gate_w), (up_hbm.at[0], up_w)])
    loads.wait(2)
    for at, size in units:
        cols = slice(at, at + size)
        pre_ref[:, cols] = dot(x_ref[...], gate_w[:, cols])
    loads.wait()
    for at, size in units:
        cols = slice(at, at + size)
        silu_ref[:, cols], slope_ref[:, cols], hidden_ref[:, cols] = activations(
            pre_ref[:, cols], dot(x_ref[...], up_w[:, cols])
        )


def other_kernel(which_ref, x_ref, gate_w, up_w, silu_ref, slope_ref, hidden_t, x_t):
    @pl.when(pl.program_id(0) == 0)
    def _():
        share = x_t.shape[0]
        x_t[...] = x_ref[:, pl.ds(pl.multiple_of(which_ref[0] * share, LANES), share)].T

    silu, slope, hidden = activations(dot(x_ref[...], gate_w[0]), dot(x_ref[...], up_w[0]))
    silu_ref[...] = silu
    slope_ref[...] = slope
    hidden_t[...] = hidden.T


def input_kernel(
    dy_ref,
    silu_ref,
    slope_ref,
    hidden_ref,
    gate_hbm,
    up_hbm,
    down_hbm,
    back_hbm,
    pre_hbm,
    up_grad_hbm,
    both_w,
    down_w,
    back_ref,
    both_ref,
    sems,
    store_sems,
):
    units = down_w.shape[0]
    loads = Loads(
        sems,
        [
            (down_hbm.at[0], down_w),
            (gate_hbm.at[0], both_w.at[:, :units]),
            (up_hbm.at[0], both_w.at[:, units:]),
        ],
    )
    gate_grad = jnp.zeros((dy_ref.shape[0], 1), F32)
    loads.wait()
    for at, size in chunks(units, 384):
        cols = slice(at, at + size)
        hidden_grad = dot(dy_ref[...], down_w[cols, :], NT)
        gate_grad += jnp.sum(hidden_ref[:, cols].astype(F32) * hidden_grad, axis=1, keepdims=True)
        both_ref[:, units + at : units + at + size] = (
            hidden_grad * silu_ref[:, cols].astype(F32)
        ).astype(BF16)
        both_ref[:, cols] = (hidden_grad * slope_ref[:, cols].astype(F32)).astype(BF16)
    stores = Stores(store_sems)
    stores.start(both_ref.at[:, :units], pre_hbm)
    stores.start(both_ref.at[:, units:], up_grad_hbm)
    gate_rows = last_rows_of_slots(gate_grad)
    loads.wait(2)
    for at, size in chunks(back_ref.shape[1], 512):
        part = dot(both_ref[...], both_w[at : at + size, :], NT)
        if at == 0:
            back_ref[:, :LANES] = (part[:, :LANES] + gate_rows).astype(BF16)
            back_ref[:, LANES:size] = part[:, LANES:].astype(BF16)
        else:
            back_ref[:, at : at + size] = part.astype(BF16)
        cols = pl.ds(at, size)
        stores.start(back_ref.at[:, cols], back_hbm.at[:, cols])
    stores.wait()


def own_kernel(
    which_ref, dy_ref, hidden_ref, x_ref, pre_ref, up_ref, gate_sum, up_sum, down_sum
):
    share = gate_sum.shape[0]
    half = pl.ds(pl.multiple_of(which_ref[0] * share, LANES), share)
    scaled_dy = dy_ref[:, half]
    hidden_t = hidden_ref[...].T
    for at, size in chunks(hidden_t.shape[0], 256):
        some = slice(at, at + size)
        down_sum[some, :] = dot(hidden_t[some, :], scaled_dy).astype(down_sum.dtype)
    x_t = x_ref[:, half].T
    for at, size in chunks(share, 256):
        some = slice(at, at + size)
        gate_sum[some, :] = dot(x_t[some, :], pre_ref[...]).astype(gate_sum.dtype)
        up_sum[some, :] = dot(x_t[some, :], up_ref[...]).astype(up_sum.dtype)


def weight_kernel(
    which_ref,
    dy_hbm,
    down_hbm,
    silu_hbm,
    slope_hbm,
    hidden_hbm,
    x_hbm,
    gate_sum_hbm,
    up_sum_hbm,
    down_sum_hbm,
    gate_hbm,
    up_hbm,
    down_out_hbm,
    dy_ref,
    down_w,
    silu_ref,
    slope_ref,
    hidden_t,
    x_t,
    gate_sum,
    up_sum,
    down_sum,
    pre_ref,
    up_ref,
    gate_out,
    up_out,
    down_out,
    sems,
    store_sems,
):
    units, share = down_sum.shape
    many, few = chunks(units, 256), chunks(share, 256)
    loads = Loads(
        sems,
        [
            (dy_hbm, dy_ref),
            (down_hbm.at[0], down_w),
            (silu_hbm, silu_ref),
            (slope_hbm, slope_ref),
            (hidden_hbm, hidden_t),
            (down_sum_hbm, down_sum),
            (x_hbm, x_t),
            (gate_sum_hbm, gate_sum),
            (up_sum_hbm, up_sum),
        ],
    )
    stores = Stores(store_sems)
    half = pl.ds(pl.multiple_of(which_ref[0] * share, LANES), share)
    loads.wait(4)
    for at, size in many:
        cols = slice(at, at + size)
        hidden_grad = dot(dy_ref[...], down_w[cols, :], NT)
        up_ref[:, cols] = (hidden_grad * silu_ref[:, cols].astype(F32)).astype(BF16)
        pre_ref[:, cols] = (hidden_grad * slope_ref[:, cols].astype(F32)).astype(BF16)
    loads.wait(5)
    for at, size in many:
        cols = pl.ds(at, size)
        down = down_sum[cols, :].astype(F32) + dot(hidden_t[cols, :], dy_ref[:, half])
        down_out[cols, :] = down.astype(down_out.dtype)
        stores.start(down_out.at[cols], down_out_hbm.at[0, cols])
    for at, size in few:
        some = pl.ds(at, size)
        gate_part = gate_sum[some, :].astype(F32) + dot(x_t[some, :], pre_ref[...])
        gate_out[some, :] = gate_part.astype(gate_out.dtype)
        stores.start(gate_out.at[some], gate_hbm.at[0, some])
        up_part = up_sum[some, :].astype(F32) + dot(x_t[some, :], up_ref[...])
        up_out[some, :] = up_part.astype(up_out.dtype)
        stores.start(up_out.at[some], up_hbm.at[0, some])
    stores.wait()


def combine_kernel(
    ids_ref, inverse_ref, place_ref, back_ref, tokens_hbm, gates_ref, tokens_ref, store_sems
):
    place = place_ref[...]
    stores = Stores(store_sems)
    for at, size in chunks(back_ref.shape[1], 512):
        cols = pl.ds(at, size)
        tokens_ref[:, at : at + size] = dot(place, back_ref[:, at : at + size]).astype(BF16)
        stores.start(tokens_ref.at[:, cols], tokens_hbm.at[:, cols])
    tok_rows, rows = place.shape
    experts = rows // SLOT
    last = iota((experts, rows), 1) == iota((experts, rows), 0) * SLOT + (SLOT - 1)
    grads = dot(last.astype(BF16), back_ref[:, :LANES]).astype(BF16)
    lane = (iota((LANES, rows), 0) == iota((LANES, rows), 1) % SLOT).astype(BF16)
    owner = iota((experts, rows), 1) // SLOT == iota((experts, rows), 0)
    by_slot = jnp.where(owner, dot(grads, lane), 0.0).astype(BF16)
    by_expert = dot(by_slot, place, NT)
    expert = iota((experts, tok_rows), 0)
    for k in range(ids_ref.shape[0]):
        own = jnp.where(ids_ref[k : k + 1, :] == expert, by_expert, 0.0)
        grad = jnp.sum(own, axis=0, keepdims=True) * inverse_ref[k : k + 1, :]
        gates_ref[k : k + 1, :] = grad.astype(BF16)
    stores.wait()


def body(tokens, out_grad, expert_ids, gate_vals, w_gate, w_up, w_down):
    expert_count = lax.axis_size("expert")
    groups = lax.axis_size("dp")
    tok_rows, features = tokens.shape
    top_count = expert_ids.shape[1]
    units = w_gate.shape[2]
    rows = expert_count * SLOT
    share = features // groups
    work = 2 * rows * features * units
    wide, many, few = (len(chunks(size, at)) for size, at in ((features, 512), (units, 256), (share, 256)))
    which = lax.axis_index("dp").reshape(1).astype(jnp.int32)
    ids = expert_ids.T
    near = pltpu.VMEM if rows * (2 * features + units) * 2 < 5 * 1024 * 1024 // 2 else None

    def exchange(send):
        return lax.all_to_all(
            send.reshape(expert_count, SLOT, features),
            "expert",
            split_axis=0,
            concat_axis=0,
            tiled=True,
        ).reshape(rows, features)

    def from_group(value, step):
        return lax.ppermute(value, "dp", [(i, (i + step) % groups) for i in range(groups)])

    def entire(shape):
        return pl.BlockSpec(shape, lambda i: (0,) * len(shape))

    send_x, key = call(
        route_kernel,
        (
            shaped((rows, features), BF16),
            shaped((expert_count, tok_rows), BF16, near),
        ),
        2 * rows * tok_rows * features,
        4 * rows * features,
        in_specs=[IN_HBM] * 2,
        out_specs=(IN_HBM, IN_VMEM),
        scratch_shapes=[
            pltpu.VMEM((top_count, tok_rows), jnp.int32),
            pltpu.VMEM((tok_rows, features), BF16),
            pltpu.VMEM((rows, features), BF16),
            pltpu.SemaphoreType.DMA((2,)),
            pltpu.SemaphoreType.DMA((wide,)),
        ],
        name="route",
    )(ids, tokens)
    rows_x = exchange(send_x)
    send_dy, place, ids, inverse = call(
        gather_kernel,
        (
            shaped((rows, features), BF16),
            shaped((tok_rows, rows), BF16, near),
            shaped((top_count, tok_rows), jnp.int32, near),
            shaped((top_count, tok_rows), F32, near),
        ),
        2 * rows * tok_rows * features,
        4 * rows * features,
        {2: near},
        in_specs=[IN_VMEM] * 3 + [IN_HBM],
        out_specs=(IN_HBM, IN_VMEM, IN_VMEM, IN_VMEM),
        scratch_shapes=[
            pltpu.VMEM((tok_rows, features), BF16),
            pltpu.VMEM((rows, features), BF16),
            pltpu.SemaphoreType.DMA((1,)),
            pltpu.SemaphoreType.DMA((wide,)),
        ],
        name="gather",
    )(ids, gate_vals.T, key, out_grad)
    rows_dy = exchange(send_dy)
    silu, slope, hidden, rows_x = call(
        forward_kernel,
        (
            shaped((rows, units), BF16, near),
            shaped((rows, units), BF16, near),
            shaped((rows, units), BF16, near),
            shaped((rows, features), BF16),
        ),
        WEIGH * 2 * work,
        4 * features * units + 2 * rows * features + 10 * rows * units,
        in_specs=[IN_HBM] * 3,
        out_specs=(IN_VMEM,) * 3 + (IN_HBM,),
        scratch_shapes=[
            pltpu.VMEM((rows, features), BF16),
            pltpu.VMEM((features, units), BF16),
            pltpu.VMEM((features, units), BF16),
            pltpu.VMEM((rows, units), F32),
            pltpu.SemaphoreType.DMA((3,)),
        ],
        input_output_aliases={0: 3},
        name="forward",
    )(rows_x, w_gate, w_up)
    back, pre_grad, up_grad = call(
        input_kernel,
        (
            shaped((rows, features), BF16),
            shaped((rows, units), BF16),
            shaped((rows, units), BF16),
        ),
        3 * work,
        6 * features * units + 4 * rows * features + 10 * rows * units,
        {0: near, 1: near, 2: near, 3: near},
        in_specs=[IN_VMEM] * 4 + [IN_HBM] * 3,
        out_specs=(IN_HBM,) * 3,
        scratch_shapes=[
            pltpu.VMEM((features, 2 * units), BF16),
            pltpu.VMEM((units, features), BF16),
            pltpu.VMEM((rows, features), BF16),
            pltpu.VMEM((rows, 2 * units), BF16),
            pltpu.SemaphoreType.DMA((3,)),
            pltpu.SemaphoreType.DMA((2 + wide,)),
        ],
        name="input_rows",
    )(rows_dy, silu, slope, hidden, w_gate, w_up, w_down)
    back = exchange(back)

    sums = call(
        own_kernel,
        (
            shaped((share, units), BF16),
            shaped((share, units), BF16),
            shaped((units, share), BF16),
        ),
        work // 4,
        2 * rows * features + 12 * share * units,
        {0: None, 1: near, 2: near},
        in_specs=[IN_SMEM, IN_VMEM, IN_VMEM]
        + [entire((rows, features))]
        + [entire((rows, units))] * 2,
        out_specs=(entire((share, units)), entire((share, units)), entire((units, share))),
        grid=(1,),
        name="own_grads",
    )(which, rows_dy, hidden, rows_x, pre_grad, up_grad)
    tiled = pl.BlockSpec((rows, 256), lambda i: (0, i))
    weight = pl.BlockSpec((1, features, 256), lambda i: (0, 0, i))
    for step in range(1, groups):
        other_x = from_group(rows_x, step)
        other_dy = from_group(rows_dy, step)
        held = call(
            other_kernel,
            (
                shaped((rows, units), BF16),
                shaped((rows, units), BF16),
                shaped((units, rows), BF16),
                shaped((share, rows), BF16),
            ),
            WEIGH * 2 * work,
            4 * features * units + 2 * rows * features + 10 * rows * units,
            {0: None},
            grid=(many,),
            in_specs=[IN_SMEM, entire((rows, features)), weight, weight],
            out_specs=(
                tiled,
                tiled,
                pl.BlockSpec((256, rows), lambda i: (i, 0)),
                entire((share, rows)),
            ),
            name="other_forward",
        )(which, other_x, w_gate, w_up)
        kind = BF16 if step == groups - 1 else F32
        sums = call(
            weight_kernel,
            (
                shaped((1, share, units), kind),
                shaped((1, share, units), kind),
                shaped((1, units, share), kind),
            ),
            WEIGH * 4 * work,
            2 * features * units + 2 * rows * features + 24 * share * units,
            {0: None},
            in_specs=[IN_SMEM] + [IN_HBM] * 9,
            out_specs=(IN_HBM,) * 3,
            scratch_shapes=[
                pltpu.VMEM((rows, features), BF16),
                pltpu.VMEM((units, features), BF16),
                pltpu.VMEM((rows, units), BF16),
                pltpu.VMEM((rows, units), BF16),
                pltpu.VMEM((units, rows), BF16),
                pltpu.VMEM((share, rows), BF16),
                pltpu.VMEM((share, units), sums[0].dtype),
                pltpu.VMEM((share, units), sums[1].dtype),
                pltpu.VMEM((units, share), sums[2].dtype),
                pltpu.VMEM((rows, units), BF16),
                pltpu.VMEM((rows, units), BF16),
                pltpu.VMEM((share, units), kind),
                pltpu.VMEM((share, units), kind),
                pltpu.VMEM((units, share), kind),
                pltpu.SemaphoreType.DMA((9,)),
                pltpu.SemaphoreType.DMA((many + 2 * few,)),
            ],
            name="weight_grads",
        )(which, other_dy, w_down, *held, *[value.reshape(value.shape[-2:]) for value in sums])
    d_gate, d_up, d_down = sums

    d_tokens, d_gates = call(
        combine_kernel,
        (
            shaped(tokens.shape, BF16),
            shaped((top_count, tok_rows), BF16),
        ),
        2 * rows * tok_rows * features,
        4 * rows * features,
        {0: near, 1: near, 2: near, 3: near},
        in_specs=[IN_VMEM] * 4,
        out_specs=(IN_HBM, IN_VMEM),
        scratch_shapes=[
            pltpu.VMEM((tok_rows, features), BF16),
            pltpu.SemaphoreType.DMA((wide,)),
        ],
        name="combine",
    )(ids, inverse, place, back)
    return d_tokens, d_gates.T, d_gate, d_up, d_down


def solution(mesh):
    in_specs = (
        P(("dp", "expert"), None),
        P(("dp", "expert"), None),
        P(("dp", "expert"), None),
        P(("dp", "expert"), None),
        P("expert", None, None),
        P("expert", None, None),
        P("expert", None, None),
    )
    out_specs = (
        P(("dp", "expert"), None),
        P(("dp", "expert"), None),
        P("expert", "dp", None),
        P("expert", "dp", None),
        P("expert", None, "dp"),
    )
    return jax.shard_map(body, mesh=mesh, in_specs=in_specs, out_specs=out_specs, check_vma=False)
```
